32 devices in a mesh: row: 8 (over z, y), col: 4 (over x, core).
Axes of the slice: x: 2, y: 2, z: 4, core: 2. Of those that a mesh axis runs over, the one named last changes fastest.
Arguments:
- laplacian: float32 [23040, 23040], P('row', 'col'), may hold values from -1 to 1.12, as said below
- block: float32 [23040, 256], P(('row', 'col')), may hold values from -6 to 6
- bounds: float32 [2], replicated, may hold values from 0.25 to 2.1, as said below
Outputs:
- filtered: float32 [23040, 256], P(('row', 'col'))
- rayleigh: float32 [256, 256], replicated
The draws below stay inside these ranges and needn't reach their ends.
Inputs may be any that keep to these rules, and one draw needn't show every extreme that they name: laplacian is symmetric; its diagonal entries lie in 0.88 to 1.12 and its other entries have magnitude at most 1.14 / sqrt(23040). bounds[0] lies in 0.25 to 0.40 and bounds[1] in 1.95 to 2.10.
All inputs are finite; a program needn't handle non-finite values.
Results may differ from the reference program's by a relative error of at most 0.00025.
Values sent between devices are 32-bit elements; how exact they have to be, the bound alone decides.
No kernel may reach another device: no remote copies, remote signals or barrier semaphores. Data moves between devices by JAX's collectives and lax.ppermute only.
A program may use at most 128 MiB of HBM per device.

```python
import math
import jax
import jax.numpy as jnp
from jax import lax

K = 256
N = 23040


def draw_laplacian(key, part):
    first_key, second_key = jax.random.split(key)
    spread = 1.04 / math.sqrt(N)
    diagonal_spread = 0.05
    entries = jax.random.uniform(first_key, (N, N), jnp.float32, -spread, spread)
    symmetric = (entries + entries.T) * 0.5
    diagonal = 1.0 + jax.random.uniform(second_key, (N,), jnp.float32, -diagonal_spread, diagonal_spread)
    positions = jnp.arange(N)
    return symmetric.at[positions, positions].set(diagonal)


def draw_bounds(key, part):
    values = jax.random.uniform(key, (2,), jnp.float32, 0.0, 1.0)
    return jnp.stack([0.25 + 0.15 * values[0], 1.95 + 0.15 * values[1]])


def steps_of(own_key, extent, cuts, low, largest):
    gain, own = 1.0, jax.random.fold_in(own_key, 6)
    for dim, shards_of in cuts:
        heights = jnp.exp(jax.random.uniform(jax.random.fold_in(own, dim), (shards_of,), jnp.float32, low / len(cuts), largest / len(cuts)))
        gain = gain * jnp.repeat(heights, extent[dim] // shards_of).reshape([-1 if axis == dim else 1 for axis in range(len(extent))])
    return gain


def centred(own_key, dims, scale, limit, cuts=(), dtype=jnp.bfloat16):
    drawn = scale * jax.random.normal(own_key, dims, jnp.float32)
    if cuts:
        drawn = drawn * steps_of(own_key, dims, cuts, -0.22, 0.18)
    return jnp.clip(drawn, -limit, limit).astype(dtype)


def setup_inputs(seed: int = 0) -> dict:
    seeds = jax.random.split(jax.random.key(seed), 4)
    return {
        "laplacian": draw_laplacian(jax.random.fold_in(seeds[3], 71), 0),
        "block": centred(seeds[1], (N, K), 1.0, 6.0, ((0, 32),), jnp.float32),
        "bounds": draw_bounds(jax.random.fold_in(seeds[3], 71), 0),
    }


def reference(laplacian, block, bounds):
    lower_bound = bounds[0]
    upper_bound = bounds[1]
    center = (upper_bound + lower_bound) * 0.5
    half_width = (upper_bound - lower_bound) * 0.5

    def shifted_product(vectors):
        return jnp.dot(laplacian.astype(jnp.float32), vectors.astype(jnp.float32), precision=lax.Precision.HIGHEST, preferred_element_type=jnp.float32) - center * vectors
    previous = block
    current = shifted_product(block) / half_width
    for degree_step in range(3):
        following = 2.0 / half_width * shifted_product(current) - previous
        previous = current
        current = following
    filtered = current
    image_full = shifted_product(filtered)
    gram = jnp.dot(filtered.T.astype(jnp.float32), filtered.astype(jnp.float32), precision=lax.Precision.HIGHEST, preferred_element_type=jnp.float32)
    projected = jnp.dot(filtered.T.astype(jnp.float32), image_full.astype(jnp.float32), precision=lax.Precision.HIGHEST, preferred_element_type=jnp.float32) + center * gram
    projected = (projected + projected.T) * 0.5
    factor = jnp.linalg.cholesky(gram)
    first_solve = jax.scipy.linalg.solve_triangular(factor, projected, lower=True)
    rayleigh = jax.scipy.linalg.solve_triangular(factor, first_solve.T, lower=True)
    return (filtered, rayleigh)
```

```python
import functools

import jax
import jax.numpy as jnp
from jax import lax
from jax.experimental import pallas as pl
from jax.experimental.pallas import tpu as pltpu
from jax.sharding import PartitionSpec as P

F32 = jnp.float32
BF16 = jnp.bfloat16
LANES = 128
NT = (((1,), (1,)), ((), ()))
NN = (((1,), (0,)), ((), ()))
BOTH = ("row", "col")
RING = (0, 2, 4, 6, 7, 5, 3, 1)
RING_AT = tuple(RING.index(r) for r in range(8))

dot32 = functools.partial(lax.dot_general, preferred_element_type=F32)
dot_exact = functools.partial(
    lax.dot_general, precision=lax.Precision.HIGHEST, preferred_element_type=F32
)


def split(values):
    high = values.astype(BF16)
    return high, (values - high.astype(F32)).astype(BF16)


def pick(table, index):
    return jnp.asarray(table, jnp.int32)[index]


def after(value, *others):
    return lax.optimization_barrier((value, others))[0]


SLOTS = 3


def stream(source_ref, slots, sems, steps, corner, use):
    _, height, width = slots.shape

    def copy(step):
        row0, col0 = corner(step)
        slot = lax.rem(step, SLOTS)
        rows = pl.ds(pl.multiple_of(row0, 8), height)
        cols = pl.ds(pl.multiple_of(col0, LANES), width)
        return pltpu.make_async_copy(source_ref.at[rows, cols], slots.at[slot], sems.at[slot])

    for step in range(min(SLOTS - 1, steps)):
        copy(jnp.int32(step)).start()

    def one(step, carry):
        copy(step).wait()

        @pl.when(step + SLOTS - 1 < steps)
        def _():
            copy(step + SLOTS - 1).start()

        use(step, lax.rem(step, SLOTS))
        return carry

    lax.fori_loop(0, steps, one, 0)


def unit_start(place, aways, index, blocks):
    away = jnp.int32(aways[0])
    for i, a in enumerate(aways[1:], 1):
        away = jnp.where(index == i, a, away)
    return lax.rem(place + away + 8, 8) * blocks // 8 * LANES


def minus_center(block, center, delta):
    rows = lax.broadcasted_iota(jnp.int32, block.shape, 0)
    cols = lax.broadcasted_iota(jnp.int32, block.shape, 1)
    return block - jnp.where(rows - cols == delta, center, 0.0)


def with_center(slots, slot, center, row0, col0, offset, use):
    _, height, width = slots.shape
    hit = (offset >= 0) & (row0 + offset < col0 + width) & (row0 + offset + height > col0)

    @pl.when(hit)
    def _():
        use(minus_center(slots[slot], center, col0 - row0 - offset))

    @pl.when(jnp.logical_not(hit))
    def _():
        use(slots[slot])


VMEM = pl.BlockSpec(memory_space=pltpu.VMEM)
SMEM = pl.BlockSpec(memory_space=pltpu.SMEM)
ANY = pl.BlockSpec(memory_space=pl.ANY)


def kernel_params(count, chunks, depth, width, vectors):
    return dict(
        compiler_params=pltpu.CompilerParams(vmem_limit_bytes=56 * 2**20),
        cost_estimate=pl.CostEstimate(
            flops=6 * count * chunks * depth * width * vectors,
            bytes_accessed=4 * count * chunks * depth * width,
            transcendentals=0,
        ),
    )


def columns_product(laplacian, scalars, center, panel, aways, depth, width, first_chunk=0, totals=None):
    count, chunks = len(aways), len(panel)
    heights = [p.shape[0] for p in panel[0]]
    vectors, per = sum(heights), len(heights)
    blocks = laplacian.shape[1] // LANES

    def kernel(scalars_ref, center_ref, tile_ref, *refs):
        pieces = refs[: per * chunks]
        total_ref = None if totals is None else refs[per * chunks]
        out_ref, slots, high_ref, low_ref, sems = refs[-5:]

        def corner(step):
            chunk = lax.bitwise_xor(first_chunk + lax.rem(step, chunks), scalars_ref[2])
            return chunk * depth, unit_start(scalars_ref[0], aways, step // chunks, blocks)

        def use(step, slot):
            chunk, unit = lax.rem(step, chunks), step // chunks

            @pl.when(step == 0)
            def _():
                for c in range(chunks):
                    at = 0
                    for q in range(per):
                        high, low = split(pieces[c * per + q][:, :depth])
                        high_ref[c, at : at + heights[q]] = high
                        low_ref[c, at : at + heights[q]] = low
                        at += heights[q]

            def add(block):
                high, low = split(block)
                z_high, z_low = high_ref[chunk], low_ref[chunk]
                term = dot32(z_high, high, NN) + dot32(z_low, high, NN) + dot32(z_high, low, NN)

                @pl.when(chunk == 0)
                def _():
                    if total_ref is None:
                        out_ref[unit] = term
                    else:
                        out_ref[unit] = total_ref[unit] + term

                @pl.when(chunk > 0)
                def _():
                    out_ref[unit] += term

            row0, col0 = corner(step)
            with_center(slots, slot, center_ref[0], row0, col0, scalars_ref[1], add)

        stream(tile_ref, slots, sems, count * chunks, corner, use)

    given = [] if totals is None else [totals]
    return pl.pallas_call(
        kernel,
        out_shape=jax.ShapeDtypeStruct((count, vectors, width), F32),
        in_specs=[SMEM, SMEM, ANY] + [VMEM] * (per * chunks + len(given)),
        out_specs=VMEM,
        scratch_shapes=[
            pltpu.VMEM((SLOTS, depth, width), F32),
            pltpu.VMEM((chunks, vectors, depth), BF16),
            pltpu.VMEM((chunks, vectors, depth), BF16),
            pltpu.SemaphoreType.DMA((SLOTS,)),
        ],
        name="columns_product",
        **kernel_params(count, chunks, depth, width, vectors),
    )(scalars, center, laplacian, *[p for pieces in panel for p in pieces], *given)


def rows_product(laplacian, scalars, center, units, aways, totals, chunks, depth, lanes):
    count, number = len(units), len(chunks)
    width = units[0][0].shape[1]
    vectors = sum(p.shape[0] for p in units[0])
    flat = [p for pieces in units for p in pieces]
    blocks = laplacian.shape[1] // LANES

    def kernel(scalars_ref, center_ref, tile_ref, *refs):
        pieces = list(refs[: len(flat)])
        total_ref = None if totals is None else refs[len(flat)]
        out_ref, slots, high_ref, low_ref, sems = refs[-5:]

        def corner(step):
            first = (chunks[0] + step // count) * depth
            return first, unit_start(scalars_ref[0], aways, lax.rem(step, count), blocks)

        def use(step, slot):
            chunk, unit = step // count, lax.rem(step, count)

            @pl.when(step == 0)
            def _():
                rest = list(pieces)
                for u in range(count):
                    at = 0
                    for _ in units[u]:
                        piece = rest.pop(0)
                        high, low = split(piece[...])
                        high_ref[u, at : at + piece.shape[0]] = high
                        low_ref[u, at : at + piece.shape[0]] = low
                        at += piece.shape[0]
                if lanes > depth:
                    out_ref[:, :, depth:] = jnp.zeros((number, vectors, lanes - depth), F32)

            def add(block):
                high, low = split(block)
                z_high, z_low = high_ref[unit], low_ref[unit]
                term = dot32(z_high, high, NT) + dot32(z_low, high, NT) + dot32(z_high, low, NT)

                @pl.when(unit == 0)
                def _():
                    if total_ref is None:
                        out_ref[chunk, :, :depth] = term
                    else:
                        out_ref[chunk, :, :depth] = total_ref[chunk, :, :depth] + term

                @pl.when(unit > 0)
                def _():
                    out_ref[chunk, :, :depth] += term

            row0, col0 = corner(step)
            with_center(slots, slot, center_ref[0], row0, col0, scalars_ref[1], add)

        stream(tile_ref, slots, sems, count * number, corner, use)

    given = [] if totals is None else [totals]
    specs = []
    if given:
        first, shape = chunks[0], (number, vectors, lanes)
        whole = totals.shape[0] == number
        specs = [VMEM if whole else pl.BlockSpec(shape, lambda _: (first, 0, 0))]
    return pl.pallas_call(
        kernel,
        grid=(1,),
        out_shape=jax.ShapeDtypeStruct((number, vectors, lanes), F32),
        in_specs=[SMEM, SMEM, ANY] + [VMEM] * len(flat) + specs,
        out_specs=VMEM,
        scratch_shapes=[
            pltpu.VMEM((SLOTS, depth, width), F32),
            pltpu.VMEM((count, vectors, width), BF16),
            pltpu.VMEM((count, vectors, width), BF16),
            pltpu.SemaphoreType.DMA((SLOTS,)),
        ],
        name="rows_product",
        **kernel_params(count, number, depth, width, vectors),
    )(scalars, center, laplacian, *flat, *given)


def inverse_factor(gram):
    size = gram.shape[0]
    tall = 32

    def kernel(gram_ref, out_ref, work):
        work[...] = gram_ref[...]
        lane = lax.broadcasted_iota(jnp.int32, (1, size), 1)
        below = lax.broadcasted_iota(jnp.int32, (tall, 1), 0)
        for first in range(0, size, tall):
            rows = work[first : first + tall]
            for q in range(0, tall, 2):
                k = first + q
                col1 = jnp.broadcast_to(rows[:, k : k + 1], rows.shape)
                col2 = jnp.broadcast_to(rows[:, k + 1 : k + 2], rows.shape)
                over1 = lax.rsqrt(col1[q : q + 1])
                cross = col2[q : q + 1] * over1
                over2 = lax.rsqrt(col2[q + 1 : q + 2] - cross * cross)
                row1 = jnp.where(lane == k, 1.0, jnp.where(lane == k + 1, 0.0, rows[q : q + 1])) * over1
                row2 = jnp.where(lane == k + 1, 1.0, jnp.where(lane == k, 0.0, rows[q + 1 : q + 2]))
                row2 = (row2 - cross * row1) * over2
                times1 = col1 * over1
                times2 = (col2 - times1 * cross) * over2
                kept = jnp.where((lane == k) | (lane == k + 1), 0.0, rows)
                rows = jnp.where(
                    below > q + 1,
                    kept - times1 * row1 - times2 * row2,
                    jnp.where(below == q, row1, jnp.where(below == q + 1, row2, rows)),
                )
            rows = jnp.where((lane > first + below) & (lane < first + tall), 0.0, rows)
            work[first : first + tall] = rows
            rest = first + tall
            if rest < size:
                update = dot_exact(rows, rows, (((0,), (0,)), ((), ())))
                done = (lane >= first) & (lane < rest)
                work[rest:] = jnp.where(done, 0.0, work[rest:]) - update[rest:]
        at_row = lax.broadcasted_iota(jnp.int32, (size, size), 0)
        at_lane = lax.broadcasted_iota(jnp.int32, (size, size), 1)
        out_ref[...] = jnp.where(at_lane <= at_row, work[...], 0.0)

    return pl.pallas_call(
        kernel,
        out_shape=jax.ShapeDtypeStruct((size, size), F32),
        in_specs=[VMEM],
        out_specs=VMEM,
        scratch_shapes=[pltpu.VMEM((size, size), F32)],
        cost_estimate=pl.CostEstimate(flops=2 * size**3, bytes_accessed=8 * size**2, transcendentals=2 * size),
        name="inverse_factor",
    )(gram)


def swap(values, axis, mask):
    size = lax.axis_size(axis)
    return lax.ppermute(values, axis, [(i, i ^ mask) for i in range(size)])


def around(values, way):
    return lax.ppermute(values, "row", [(RING[p], RING[(p + way) % 8]) for p in range(8)])


def sum_stages(partial):
    row, col = lax.axis_index("row"), lax.axis_index("col")
    stages = (("col", 1, col & 1), ("col", 2, (col >> 1) & 1), ("row", 1, row & 1))
    values = partial
    for axis, mask, bit in stages:
        half = values.shape[0] // 2
        low, high = values[:half], values[half:]
        keep = jnp.where(bit == 0, low, high)
        send = jnp.where(bit == 0, high, low)
        values = keep + swap(send, axis, mask)
        yield values
    terms = [values] + [swap(values, "row", mask) for mask in (2, 4, 6)]
    z = row >> 1
    ordered = []
    for place in range(4):
        which = z ^ place
        ordered.append(jnp.where(which == 0, terms[0], jnp.where(which == 1, terms[1], jnp.where(which == 2, terms[2], terms[3]))))
    values = (ordered[0] + ordered[1]) + (ordered[2] + ordered[3])
    yield values
    for axis, mask, bit in reversed(stages):
        other = swap(values, axis, mask)
        low = jnp.where(bit == 0, values, other)
        high = jnp.where(bit == 0, other, values)
        values = jnp.concatenate([low, high], axis=0)
        yield values


def tuned_body(laplacian, block, bounds):
    tile_rows, tile_cols = laplacian.shape
    own_rows, vectors = block.shape
    half = vectors // 2
    depth = tile_rows // 2
    lanes = -(-depth // LANES) * LANES
    row, col = lax.axis_index("row"), lax.axis_index("col")
    core, x_at = col & 1, col >> 1
    place = pick(RING_AT, row)
    blocks = tile_cols // LANES
    starts = tuple(blocks * p // 8 for p in range(9))
    width = LANES * max(b - a for a, b in zip(starts, starts[1:]))
    center = (bounds[1] + bounds[0]) * 0.5
    half_width = (bounds[1] - bounds[0]) * 0.5
    factor_two = 2.0 / half_width
    centers = center.reshape(1)
    valid = lax.broadcasted_iota(jnp.int32, (1, width), 1) < (pick(starts, place + 1) - pick(starts, place)) * LANES
    per_tile = tile_cols // tile_rows
    offset = jnp.where(row // per_tile == col, (row % per_tile) * tile_rows, -1)
    scalars, turned_scalars = (jnp.stack([place, offset, f]).astype(jnp.int32) for f in (jnp.int32(0), x_at))

    def through_columns(here, rest, scalars=scalars, before=None):
        def product(call, aways, panel, **more):
            told = scalars if before is None else after(scalars, *before(call))
            return columns_product(laplacian, told, centers, panel, aways, depth, width, **more)

        begun_far = product(0, (4,), [here])
        begun = product(0, (3, -3), [here])
        there = rest(begun_far, begun)
        panel = [here, there]
        far = product(1, (4,), [there], first_chunk=1, totals=begun_far)[0]
        right, left = around(far[:half], 1), around(far[half:], -1)
        ahead, behind = product(2, (3, -3), [there], first_chunk=1, totals=begun)
        ahead = jnp.concatenate([ahead[:half] + right, ahead[half:]], 0)
        behind = jnp.concatenate([behind[:half], behind[half:] + left], 0)
        right, left = around(ahead, 1), around(behind, -1)
        ahead, behind = product(3, (2, -2), panel)
        right, left = around(ahead + right, 1), around(behind + left, -1)
        ahead, behind, own = product(4, (1, -1, 0), panel)
        ahead, behind = ahead + right, behind + left
        return panel, (own, around(ahead, 1), around(behind, -1)), ahead

    def through_rows(unit, before):
        unit = jnp.where(valid, unit, 0.0)

        def product(aways, units, totals, chunks):
            return rows_product(laplacian, scalars, centers, units, aways, totals, chunks, depth, lanes)

        right, left = around(unit, 1), around(unit, -1)
        totals = product((0,), [[unit]], None, (0, 1))
        right, left = after(right, totals), after(left, totals)
        right2, left2 = around(right, 1), around(left, -1)
        totals = product((-1, 1), [[right], [left]], totals, (0, 1))
        right2, left2 = after(right2, totals), after(left2, totals)
        right3, left3 = around(right2, 1), around(left2, -1)
        totals = product((-2, 2), [[right2], [left2]], totals, (0, 1))
        right3, left3 = after(right3, totals), after(left3, totals)
        far = [around(right3[:half], 1), around(left3[half:], -1)]
        first = product((-3, 3), [[right3], [left3]], totals, (0,))
        first = product((4,), [far], first, (0,))[0]
        first = first[:half] + swap(first[half:], "col", 1)
        second = product((-3, 3, 4), [[right3], [left3], far], after(totals, first), (1,))[0]
        first = factor_two * (first + swap(first, "col", 2)) - before[0][0]
        second = after(second[:half] + swap(second[half:], "col", 1), first)
        second_there = swap(second, "col", 2)

        def rest(*others):
            new = after(factor_two * (second + second_there) - before[1][0], *others)
            return new, swap(new, "col", 1)

        return (first, swap(first, "col", 1)), rest

    away_block = swap(block, "col", 2)
    chip = [block, swap(block, "col", 1)]
    away_chip = [away_block, swap(away_block, "col", 1)]

    def turned(pair):
        mine, other = pair[0].T, pair[1].T
        both = jnp.where(core == 0, jnp.concatenate([mine, other], 1), jnp.concatenate([other, mine], 1))
        both = jnp.pad(both, ((0, 0), (0, lanes - depth)))
        return jnp.where(core == 0, both[:half], both[half:]), jnp.where(core == 0, both[half:], both[:half])

    here, there = turned(chip), turned(away_chip)
    panel = [(jnp.where(x_at == 0, here[0], there[0]),), (jnp.where(x_at == 0, there[0], here[0]),)]

    _, terms, _ = through_columns(here, lambda *_: there, turned_scalars)
    filter_one = sum(terms) / half_width
    panel_two, terms, _ = through_columns(*through_rows(filter_one, panel))
    filter_three = factor_two * sum(terms) - filter_one

    def straight(pieces):
        mine, other = pieces
        return jnp.where(core == 0, jnp.concatenate([mine, other], 0), jnp.concatenate([other, mine], 0))

    held = []

    def whole_panel(here, there):
        chunks = [straight(pair)[:, :depth] for pair in (here, there)]
        chunk = jnp.where(x_at == 0, chunks[0], chunks[1])
        own = jnp.where(core == 0, chunk[:, :own_rows], chunk[:, own_rows:])
        held.append(sum_stages(dot_exact(own, own, NT)))
        return chunks, own

    def before(call):
        for _ in range((0, 0, 1, 3, 3)[call]):
            held.append(next(held[0]))
        return held[-1:] if call > 1 else []

    here, rest = through_rows(filter_three, panel_two)
    got = []

    def rest_and_gram(*others):
        there = rest(*others)
        got.append(whole_panel(here, there))
        return there

    _, (image, from_left, from_right), last_sent = through_columns(here, rest_and_gram, before=before)
    panel_chunks, own = got[0]
    filtered = own.T

    lead = LANES
    padded = jnp.concatenate([jnp.zeros((vectors, lead), F32)] + panel_chunks, 1)
    part = row % per_tile
    send_from = pick(starts, 4 * part + col) * LANES - part * tile_rows + lead
    sent = lax.dynamic_slice_in_dim(padded, send_from, width, 1)
    pairs = [
        (4 * r + c, 4 * RING[4 * (r % per_tile) + c] + r // per_tile) for r in range(8) for c in range(4)
    ]
    moved = lax.ppermute(sent, BOTH, pairs)
    over = tile_rows - starts[4] * LANES
    head = lax.ppermute(
        panel_chunks[1][:, depth - over :], BOTH, [(4 * (per_tile * c), 4 * RING[4] + c) for c in range(4)]
    )
    moved = jnp.where(valid, moved + jnp.pad(head, ((0, 0), (0, width - over))), 0.0)

    gram = held[-1]
    inverse = inverse_factor(after(gram, last_sent))
    image = after(image, inverse) + from_left + from_right
    image = straight((image[:half], image[half:]))
    *_, projected = sum_stages(dot_exact(moved, image, NT))
    projected = projected + center * gram
    projected = (projected + projected.T) * 0.5
    rayleigh = dot_exact(dot_exact(inverse, projected, NN), inverse, NT)
    return (filtered, rayleigh)


def plain_body(laplacian, block, bounds):
    row_index = lax.axis_index("row")
    col_index = lax.axis_index("col")
    tile_rows, tile_cols = laplacian.shape
    center = (bounds[1] + bounds[0]) * 0.5
    half_width = (bounds[1] - bounds[0]) * 0.5
    factor_two = 2.0 / half_width
    global_rows = row_index * tile_rows + lax.broadcasted_iota(jnp.int32, (tile_rows, tile_cols), 0)
    global_cols = col_index * tile_cols + lax.broadcasted_iota(jnp.int32, (tile_rows, tile_cols), 1)
    moved_diagonal = laplacian - center * (global_rows == global_cols).astype(F32)

    def through_columns(values):
        panel = lax.all_gather(values, "col", axis=0, tiled=True)
        out = dot_exact(moved_diagonal, panel, (((0,), (0,)), ((), ())))
        return lax.psum_scatter(out, "row", scatter_dimension=0, tiled=True)

    def through_rows(values):
        panel = lax.all_gather(values, "row", axis=0, tiled=True)
        out = dot_exact(moved_diagonal, panel, NN)
        return lax.psum_scatter(out, "col", scatter_dimension=0, tiled=True)

    filter_one = through_columns(block) / half_width
    filter_two = factor_two * through_rows(filter_one) - block
    filter_three = factor_two * through_columns(filter_two) - filter_one
    filter_four = factor_two * through_rows(filter_three) - filter_two
    image = through_columns(filter_four)
    rows, cols = lax.axis_size("row"), lax.axis_size("col")
    pairs = [(i, (i % rows) * cols + i // rows) for i in range(rows * cols)]
    moved = lax.ppermute(filter_four, BOTH, pairs)
    inner = (((0,), (0,)), ((), ()))
    gram, projected = lax.psum((dot_exact(moved, moved, inner), dot_exact(moved, image, inner)), BOTH)
    projected = projected + center * gram
    projected = (projected + projected.T) * 0.5
    factor = jnp.linalg.cholesky(gram)
    first_solve = jax.scipy.linalg.solve_triangular(factor, projected, lower=True)
    rayleigh = jax.scipy.linalg.solve_triangular(factor, first_solve.T, lower=True)
    return (filter_four, rayleigh)


def solution(mesh):
    tuned = mesh.shape["row"] == 8 and mesh.shape["col"] == 4
    placed = (P("row", "col"), P(BOTH, None), P())
    return jax.shard_map(
        tuned_body if tuned else plain_body,
        mesh=mesh,
        in_specs=placed,
        out_specs=(P(BOTH, None), P()),
        check_vma=False,
    )
```

```python
import functools

import jax
import jax.numpy as jnp
from jax import lax
from jax.experimental import pallas as pl
from jax.experimental.pallas import tpu as pltpu
from jax.sharding import PartitionSpec as P

F32 = jnp.float32
BF16 = jnp.bfloat16
LANES = 128
NT = (((1,), (1,)), ((), ()))
NN = (((1,), (0,)), ((), ()))
BOTH = ("row", "col")
RING = (0, 2, 4, 6, 7, 5, 3, 1)
RING_AT = tuple(RING.index(r) for r in range(8))

dot32 = functools.partial(lax.dot_general, preferred_element_type=F32)
dot_exact = functools.partial(
    lax.dot_general, precision=lax.Precision.HIGHEST, preferred_element_type=F32
)


def split(values):
    high = values.astype(BF16)
    return high, (values - high.astype(F32)).astype(BF16)


def pick(table, index):
    return jnp.asarray(table, jnp.int32)[index]


def after(value, *others):
    return lax.optimization_barrier((value, others))[0]


SLOTS = 3
ROUND = 32


def stream(source_ref, slots, sems, steps, corner, prepare, use):
    _, height, width = slots.shape

    def copy(step):
        row0, col0 = corner(step)
        slot = lax.rem(step, SLOTS)
        rows = pl.ds(pl.multiple_of(row0, ROUND), height)
        cols = pl.ds(pl.multiple_of(col0, LANES), width)
        return pltpu.make_async_copy(source_ref.at[rows, cols], slots.at[slot], sems.at[slot])

    copy(jnp.int32(0)).start()
    prepare()
    for step in range(1, min(SLOTS - 1, steps)):
        copy(jnp.int32(step)).start()

    def one(step, carry):
        @pl.when(step + SLOTS - 1 < steps)
        def _():
            copy(step + SLOTS - 1).start()

        copy(step).wait()
        use(step, lax.rem(step, SLOTS))
        return carry

    lax.fori_loop(0, steps, one, 0)


def unit_start(place, aways, index, blocks):
    away = jnp.int32(aways[0])
    for i, a in enumerate(aways[1:], 1):
        away = jnp.where(index == i, a, away)
    return lax.rem(place + away + 8, 8) * blocks // 8 * LANES


def take_center(slots, slot, center, row0, col0, offset):
    _, height, width = slots.shape
    first = col0 - row0 - offset

    @pl.when((offset >= 0) & (first < height) & (first + width > 0))
    def _():
        rows = lax.broadcasted_iota(jnp.int32, (ROUND, LANES), 0)
        cols = lax.broadcasted_iota(jnp.int32, (ROUND, LANES), 1)

        def tile(index, carry):
            for part in range(LANES // ROUND):
                at = first + index * LANES + part * ROUND

                @pl.when((at >= 0) & (at < height))
                def _():
                    here = (slot, pl.ds(pl.multiple_of(at, ROUND), ROUND), pl.ds(pl.multiple_of(index * LANES, LANES), LANES))
                    slots[here] = slots[here] - jnp.where(rows + part * ROUND == cols, center, 0.0)

            return carry

        lax.fori_loop(0, width // LANES, tile, 0)


VMEM = pl.BlockSpec(memory_space=pltpu.VMEM)
SMEM = pl.BlockSpec(memory_space=pltpu.SMEM)
ANY = pl.BlockSpec(memory_space=pl.ANY)


def kernel_params(count, chunks, depth, width, vectors):
    return dict(
        compiler_params=pltpu.CompilerParams(vmem_limit_bytes=36 * 2**20),
        cost_estimate=pl.CostEstimate(
            flops=6 * count * chunks * depth * width * vectors,
            bytes_accessed=4 * count * chunks * depth * width,
            transcendentals=0,
        ),
    )


def bring(pieces, refs, held, sems):
    copies, rest = [], list(refs)
    for i, group in enumerate(pieces):
        at, own = 0, []
        for q, piece in enumerate(group):
            own.append(pltpu.make_async_copy(rest.pop(0), held.at[i, pl.ds(at, piece.shape[0])], sems.at[i, q]))
            at += piece.shape[0]
        copies.append(own)
    return copies


def columns_product(laplacian, scalars, center, panel, aways, depth, width, first_chunk=0, totals=None):
    count, chunks = len(aways), len(panel)
    lanes = panel[0][0].shape[1]
    vectors, per = sum(p.shape[0] for p in panel[0]), len(panel[0])
    blocks = laplacian.shape[1] // LANES
    given = [] if totals is None else [totals]

    def kernel(scalars_ref, center_ref, tile_ref, *refs):
        piece_refs, total_refs = refs[: per * chunks], refs[per * chunks : per * chunks + len(given)]
        out_ref, slots, panel_ref, high_ref, low_ref, sum_ref, total_buf, sems, in_sems, total_sem, out_sems = refs[-11:]
        copies = bring(panel, piece_refs, panel_ref, in_sems)
        more = [pltpu.make_async_copy(r, total_buf, total_sem.at[0]) for r in total_refs]

        def corner(step):
            chunk = lax.bitwise_xor(first_chunk + lax.rem(step, chunks), scalars_ref[2])
            return chunk * depth, unit_start(scalars_ref[0], aways, step // chunks, blocks)

        def prepare():
            for copy in [c for own in copies for c in own] + more:
                copy.start()

        def use(step, slot):
            chunk, unit = lax.rem(step, chunks), step // chunks
            for c in range(chunks):

                @pl.when(step == c)
                def _(c=c):
                    for copy in copies[c]:
                        copy.wait()
                    high, low = split(panel_ref[c, :, :depth])
                    high_ref[c] = high
                    low_ref[c] = low

            row0, col0 = corner(step)
            take_center(slots, slot, center_ref[0], row0, col0, scalars_ref[1])
            high, low = split(slots[slot])
            z_high, z_low = high_ref[chunk], low_ref[chunk]
            term = dot32(z_high, high, NN) + dot32(z_low, high, NN) + dot32(z_high, low, NN)

            @pl.when(chunk == 0)
            def _():
                if more:

                    @pl.when(step == 0)
                    def _():
                        for copy in more:
                            copy.wait()

                    sum_ref[unit] = total_buf[unit] + term
                else:
                    sum_ref[unit] = term

            @pl.when(chunk > 0)
            def _():
                sum_ref[unit] += term

            @pl.when(chunk == chunks - 1)
            def _():
                pltpu.make_async_copy(sum_ref.at[unit], out_ref.at[unit], out_sems.at[unit]).start()

        stream(tile_ref, slots, sems, count * chunks, corner, prepare, use)
        for unit in range(count):
            pltpu.make_async_copy(sum_ref.at[unit], out_ref.at[unit], out_sems.at[unit]).wait()

    return pl.pallas_call(
        kernel,
        out_shape=jax.ShapeDtypeStruct((count, vectors, width), F32),
        in_specs=[SMEM, SMEM, ANY] + [ANY] * (per * chunks + len(given)),
        out_specs=ANY,
        scratch_shapes=[
            pltpu.VMEM((SLOTS, depth, width), F32),
            pltpu.VMEM((chunks, vectors, lanes), F32),
            pltpu.VMEM((chunks, vectors, depth), BF16),
            pltpu.VMEM((chunks, vectors, depth), BF16),
            pltpu.VMEM((count, vectors, width), F32),
            pltpu.VMEM((count, vectors, width) if given else (1, 8, LANES), F32),
            pltpu.SemaphoreType.DMA((SLOTS,)),
            pltpu.SemaphoreType.DMA((chunks, per)),
            pltpu.SemaphoreType.DMA((1,)),
            pltpu.SemaphoreType.DMA((count,)),
        ],
        name="columns_product",
        **kernel_params(count, chunks, depth, width, vectors),
    )(scalars, center, laplacian, *[p for pieces in panel for p in pieces], *given)


def rows_product(laplacian, scalars, center, units, aways, totals, chunks, depth, lanes):
    count, number = len(units), len(chunks)
    width = units[0][0].shape[1]
    vectors = sum(p.shape[0] for p in units[0])
    per = max(len(group) for group in units)
    flat = [p for pieces in units for p in pieces]
    blocks = laplacian.shape[1] // LANES
    given = [] if totals is None else [totals]
    skip = chunks[0] if given and totals.shape[0] > number else 0

    def kernel(scalars_ref, center_ref, tile_ref, *refs):
        total_refs = refs[len(flat) : len(flat) + len(given)]
        out_ref, slots, unit_ref, high_ref, low_ref, sum_ref, total_buf, sems, in_sems, total_sems, out_sems = refs[-11:]
        copies = bring(units, refs[: len(flat)], unit_ref, in_sems)

        def total(chunk):
            return [pltpu.make_async_copy(r.at[skip + chunk], total_buf.at[chunk], total_sems.at[chunk]) for r in total_refs]

        def corner(step):
            first = (chunks[0] + step // count) * depth
            return first, unit_start(scalars_ref[0], aways, lax.rem(step, count), blocks)

        def prepare():
            for copy in [c for own in copies for c in own] + [c for i in range(number) for c in total(i)]:
                copy.start()

        def use(step, slot):
            chunk, unit = step // count, lax.rem(step, count)
            for u in range(count):

                @pl.when(step == u)
                def _(u=u):
                    for copy in copies[u]:
                        copy.wait()
                    high, low = split(unit_ref[u])
                    high_ref[u] = high
                    low_ref[u] = low
                    if u == 0 and lanes > depth:
                        sum_ref[:, :, depth:] = jnp.zeros((number, vectors, lanes - depth), F32)

            row0, col0 = corner(step)
            take_center(slots, slot, center_ref[0], row0, col0, scalars_ref[1])
            high, low = split(slots[slot])
            z_high, z_low = high_ref[unit], low_ref[unit]
            term = dot32(z_high, high, NT) + dot32(z_low, high, NT) + dot32(z_high, low, NT)

            @pl.when(unit == 0)
            def _():
                if given:
                    for copy in total(chunk):
                        copy.wait()
                    sum_ref[chunk, :, :depth] = total_buf[chunk, :, :depth] + term
                else:
                    sum_ref[chunk, :, :depth] = term

            @pl.when(unit > 0)
            def _():
                sum_ref[chunk, :, :depth] += term

            @pl.when(unit == count - 1)
            def _():
                pltpu.make_async_copy(sum_ref.at[chunk], out_ref.at[chunk], out_sems.at[chunk]).start()

        stream(tile_ref, slots, sems, count * number, corner, prepare, use)
        for chunk in range(number):
            pltpu.make_async_copy(sum_ref.at[chunk], out_ref.at[chunk], out_sems.at[chunk]).wait()

    return pl.pallas_call(
        kernel,
        out_shape=jax.ShapeDtypeStruct((number, vectors, lanes), F32),
        in_specs=[SMEM, SMEM, ANY] + [ANY] * (len(flat) + len(given)),
        out_specs=ANY,
        scratch_shapes=[
            pltpu.VMEM((SLOTS, depth, width), F32),
            pltpu.VMEM((count, vectors, width), F32),
            pltpu.VMEM((count, vectors, width), BF16),
            pltpu.VMEM((count, vectors, width), BF16),
            pltpu.VMEM((number, vectors, lanes), F32),
            pltpu.VMEM((number, vectors, lanes) if given else (1, 8, LANES), F32),
            pltpu.SemaphoreType.DMA((SLOTS,)),
            pltpu.SemaphoreType.DMA((count, per)),
            pltpu.SemaphoreType.DMA((number,)),
            pltpu.SemaphoreType.DMA((number,)),
        ],
        name="rows_product",
        **kernel_params(count, number, depth, width, vectors),
    )(scalars, center, laplacian, *flat, *given)


def inverse_factor(gram):
    size = gram.shape[0]
    tall = 32

    def kernel(gram_ref, out_ref, work):
        work[...] = gram_ref[...]
        lane = lax.broadcasted_iota(jnp.int32, (1, size), 1)
        below = lax.broadcasted_iota(jnp.int32, (tall, 1), 0)
        for first in range(0, size, tall):
            rows = work[first : first + tall]
            for q in range(0, tall, 2):
                k = first + q
                col1 = jnp.broadcast_to(rows[:, k : k + 1], rows.shape)
                col2 = jnp.broadcast_to(rows[:, k + 1 : k + 2], rows.shape)
                over1 = lax.rsqrt(col1[q : q + 1])
                cross = col2[q : q + 1] * over1
                over2 = lax.rsqrt(col2[q + 1 : q + 2] - cross * cross)
                row1 = jnp.where(lane == k, 1.0, jnp.where(lane == k + 1, 0.0, rows[q : q + 1])) * over1
                row2 = jnp.where(lane == k + 1, 1.0, jnp.where(lane == k, 0.0, rows[q + 1 : q + 2]))
                row2 = (row2 - cross * row1) * over2
                times1 = col1 * over1
                times2 = (col2 - times1 * cross) * over2
                kept = jnp.where((lane == k) | (lane == k + 1), 0.0, rows)
                rows = jnp.where(
                    below > q + 1,
                    kept - times1 * row1 - times2 * row2,
                    jnp.where(below == q, row1, jnp.where(below == q + 1, row2, rows)),
                )
            rows = jnp.where((lane > first + below) & (lane < first + tall), 0.0, rows)
            work[first : first + tall] = rows
            rest = first + tall
            if rest < size:
                update = dot_exact(rows, rows, (((0,), (0,)), ((), ())))
                done = (lane >= first) & (lane < rest)
                work[rest:] = jnp.where(done, 0.0, work[rest:]) - update[rest:]
        at_row = lax.broadcasted_iota(jnp.int32, (size, size), 0)
        at_lane = lax.broadcasted_iota(jnp.int32, (size, size), 1)
        out_ref[...] = jnp.where(at_lane <= at_row, work[...], 0.0)

    return pl.pallas_call(
        kernel,
        out_shape=jax.ShapeDtypeStruct((size, size), F32),
        in_specs=[VMEM],
        out_specs=VMEM,
        scratch_shapes=[pltpu.VMEM((size, size), F32)],
        cost_estimate=pl.CostEstimate(flops=2 * size**3, bytes_accessed=8 * size**2, transcendentals=2 * size),
        name="inverse_factor",
    )(gram)


def swap(values, axis, mask):
    size = lax.axis_size(axis)
    return lax.ppermute(values, axis, [(i, i ^ mask) for i in range(size)])


def around(values, way):
    return lax.ppermute(values, "row", [(RING[p], RING[(p + way) % 8]) for p in range(8)])


def sum_stages(partial):
    row, col = lax.axis_index("row"), lax.axis_index("col")
    stages = (("col", 1, col & 1), ("col", 2, (col >> 1) & 1), ("row", 1, row & 1))
    values = partial
    for axis, mask, bit in stages:
        half = values.shape[0] // 2
        low, high = values[:half], values[half:]
        keep = jnp.where(bit == 0, low, high)
        send = jnp.where(bit == 0, high, low)
        values = keep + swap(send, axis, mask)
        yield values
    terms = [values] + [swap(values, "row", mask) for mask in (2, 4, 6)]
    z = row >> 1
    ordered = []
    for place in range(4):
        which = z ^ place
        ordered.append(jnp.where(which == 0, terms[0], jnp.where(which == 1, terms[1], jnp.where(which == 2, terms[2], terms[3]))))
    values = (ordered[0] + ordered[1]) + (ordered[2] + ordered[3])
    yield values
    for axis, mask, bit in reversed(stages):
        other = swap(values, axis, mask)
        low = jnp.where(bit == 0, values, other)
        high = jnp.where(bit == 0, other, values)
        values = jnp.concatenate([low, high], axis=0)
        yield values


def tuned_body(laplacian, block, bounds):
    tile_rows, tile_cols = laplacian.shape
    own_rows, vectors = block.shape
    half = vectors // 2
    depth = tile_rows // 2
    lanes = -(-depth // LANES) * LANES
    row, col = lax.axis_index("row"), lax.axis_index("col")
    core, x_at = col & 1, col >> 1
    place = pick(RING_AT, row)
    blocks = tile_cols // LANES
    starts = tuple(blocks * p // 8 for p in range(9))
    width = LANES * max(b - a for a, b in zip(starts, starts[1:]))
    center = (bounds[1] + bounds[0]) * 0.5
    half_width = (bounds[1] - bounds[0]) * 0.5
    factor_two = 2.0 / half_width
    centers = center.reshape(1)
    valid = lax.broadcasted_iota(jnp.int32, (1, width), 1) < (pick(starts, place + 1) - pick(starts, place)) * LANES
    per_tile = tile_cols // tile_rows
    offset = jnp.where(row // per_tile == col, (row % per_tile) * tile_rows, -1)
    scalars, turned_scalars = (jnp.stack([place, offset, f]).astype(jnp.int32) for f in (jnp.int32(0), x_at))

    def through_columns(here, rest, scalars=scalars, before=None):
        def product(call, aways, panel, **more):
            told = scalars if before is None else after(scalars, *before(call))
            return columns_product(laplacian, told, centers, panel, aways, depth, width, **more)

        begun_far = product(0, (4,), [here])
        begun = product(0, (3, -3), [here])
        there = rest(begun_far, begun)
        panel = [here, there]
        far = product(1, (4,), [there], first_chunk=1, totals=begun_far)[0]
        right, left = around(far[:half], 1), around(far[half:], -1)
        ahead, behind = product(2, (3, -3), [there], first_chunk=1, totals=begun)
        ahead = jnp.concatenate([ahead[:half] + right, ahead[half:]], 0)
        behind = jnp.concatenate([behind[:half], behind[half:] + left], 0)
        right, left = around(ahead, 1), around(behind, -1)
        ahead, behind = product(3, (2, -2), panel)
        right, left = around(ahead + right, 1), around(behind + left, -1)
        ahead, behind, own = product(4, (1, -1, 0), panel)
        ahead, behind = ahead + right, behind + left
        return panel, (own, around(ahead, 1), around(behind, -1)), ahead

    def through_rows(unit, before):
        unit = jnp.where(valid, unit, 0.0)

        def product(aways, units, totals, chunks):
            return rows_product(laplacian, scalars, centers, units, aways, totals, chunks, depth, lanes)

        right, left = around(unit, 1), around(unit, -1)
        totals = product((0,), [[unit]], None, (0, 1))
        right, left = after(right, totals), after(left, totals)
        right2, left2 = around(right, 1), around(left, -1)
        totals = product((-1, 1), [[right], [left]], totals, (0, 1))
        right2, left2 = after(right2, totals), after(left2, totals)
        right3, left3 = around(right2, 1), around(left2, -1)
        totals = product((-2, 2), [[right2], [left2]], totals, (0, 1))
        right3, left3 = after(right3, totals), after(left3, totals)
        far = [around(right3[:half], 1), around(left3[half:], -1)]
        first = product((-3, 3), [[right3], [left3]], totals, (0,))
        first = product((4,), [far], first, (0,))[0]
        first = first[:half] + swap(first[half:], "col", 1)
        second = product((-3, 3, 4), [[right3], [left3], far], after(totals, first), (1,))[0]
        first = factor_two * (first + swap(first, "col", 2)) - before[0][0]
        second = after(second[:half] + swap(second[half:], "col", 1), first)
        second_there = swap(second, "col", 2)

        def rest(*others):
            new = after(factor_two * (second + second_there) - before[1][0], *others)
            return new, swap(new, "col", 1)

        return (first, swap(first, "col", 1)), rest

    away_block = swap(block, "col", 2)

    def turned(pair):
        mine, other = pair[0].T, pair[1].T
        both = jnp.where(core == 0, jnp.concatenate([mine, other], 1), jnp.concatenate([other, mine], 1))
        both = jnp.pad(both, ((0, 0), (0, lanes - depth)))
        return jnp.where(core == 0, both[:half], both[half:]), jnp.where(core == 0, both[half:], both[:half])

    def rest(*others):
        away = after(away_block, *others)
        return turned([away, swap(away, "col", 1)])

    here = turned([block, swap(block, "col", 1)])
    (_, there), terms, _ = through_columns(here, rest, turned_scalars)
    panel = [(jnp.where(x_at == 0, here[0], there[0]),), (jnp.where(x_at == 0, there[0], here[0]),)]
    filter_one = sum(terms) / half_width
    panel_two, terms, _ = through_columns(*through_rows(filter_one, panel))
    filter_three = factor_two * sum(terms) - filter_one

    def straight(pieces):
        mine, other = pieces
        return jnp.where(core == 0, jnp.concatenate([mine, other], 0), jnp.concatenate([other, mine], 0))

    held = []

    def whole_panel(here, there):
        chunks = [straight(pair)[:, :depth] for pair in (here, there)]
        chunk = jnp.where(x_at == 0, chunks[0], chunks[1])
        own = jnp.where(core == 0, chunk[:, :own_rows], chunk[:, own_rows:])
        held.append(sum_stages(dot_exact(own, own, NT)))
        return chunks, own

    def before(call):
        for _ in range((0, 0, 1, 3, 3)[call]):
            held.append(next(held[0]))
        return held[-1:] if call > 1 else []

    here, rest = through_rows(filter_three, panel_two)
    got = []

    def rest_and_gram(*others):
        there = rest(*others)
        got.append(whole_panel(here, there))
        return there

    _, (image, from_left, from_right), last_sent = through_columns(here, rest_and_gram, before=before)
    panel_chunks, own = got[0]
    filtered = own.T

    lead = LANES
    padded = jnp.concatenate([jnp.zeros((vectors, lead), F32)] + panel_chunks, 1)
    part = row % per_tile
    send_from = pick(starts, 4 * part + col) * LANES - part * tile_rows + lead
    sent = lax.dynamic_slice_in_dim(padded, send_from, width, 1)
    pairs = [
        (4 * r + c, 4 * RING[4 * (r % per_tile) + c] + r // per_tile) for r in range(8) for c in range(4)
    ]
    moved = lax.ppermute(sent, BOTH, pairs)
    over = tile_rows - starts[4] * LANES
    head = lax.ppermute(
        panel_chunks[1][:, depth - over :], BOTH, [(4 * (per_tile * c), 4 * RING[4] + c) for c in range(4)]
    )
    moved = jnp.where(valid, moved + jnp.pad(head, ((0, 0), (0, width - over))), 0.0)

    gram = held[-1]
    inverse = inverse_factor(after(gram, last_sent))
    image = after(image, inverse) + from_left + from_right
    image = straight((image[:half], image[half:]))
    *_, projected = sum_stages(dot_exact(moved, image, NT))
    projected = projected + center * gram
    projected = (projected + projected.T) * 0.5
    rayleigh = dot_exact(dot_exact(inverse, projected, NN), inverse, NT)
    return (filtered, rayleigh)


def plain_body(laplacian, block, bounds):
    row_index = lax.axis_index("row")
    col_index = lax.axis_index("col")
    tile_rows, tile_cols = laplacian.shape
    center = (bounds[1] + bounds[0]) * 0.5
    half_width = (bounds[1] - bounds[0]) * 0.5
    factor_two = 2.0 / half_width
    global_rows = row_index * tile_rows + lax.broadcasted_iota(jnp.int32, (tile_rows, tile_cols), 0)
    global_cols = col_index * tile_cols + lax.broadcasted_iota(jnp.int32, (tile_rows, tile_cols), 1)
    moved_diagonal = laplacian - center * (global_rows == global_cols).astype(F32)

    def through_columns(values):
        panel = lax.all_gather(values, "col", axis=0, tiled=True)
        out = dot_exact(moved_diagonal, panel, (((0,), (0,)), ((), ())))
        return lax.psum_scatter(out, "row", scatter_dimension=0, tiled=True)

    def through_rows(values):
        panel = lax.all_gather(values, "row", axis=0, tiled=True)
        out = dot_exact(moved_diagonal, panel, NN)
        return lax.psum_scatter(out, "col", scatter_dimension=0, tiled=True)

    filter_one = through_columns(block) / half_width
    filter_two = factor_two * through_rows(filter_one) - block
    filter_three = factor_two * through_columns(filter_two) - filter_one
    filter_four = factor_two * through_rows(filter_three) - filter_two
    image = through_columns(filter_four)
    rows, cols = lax.axis_size("row"), lax.axis_size("col")
    pairs = [(i, (i % rows) * cols + i // rows) for i in range(rows * cols)]
    moved = lax.ppermute(filter_four, BOTH, pairs)
    inner = (((0,), (0,)), ((), ()))
    gram, projected = lax.psum((dot_exact(moved, moved, inner), dot_exact(moved, image, inner)), BOTH)
    projected = projected + center * gram
    projected = (projected + projected.T) * 0.5
    factor = jnp.linalg.cholesky(gram)
    first_solve = jax.scipy.linalg.solve_triangular(factor, projected, lower=True)
    rayleigh = jax.scipy.linalg.solve_triangular(factor, first_solve.T, lower=True)
    return (filter_four, rayleigh)


def solution(mesh):
    tuned = mesh.shape["row"] == 8 and mesh.shape["col"] == 4
    placed = (P("row", "col"), P(BOTH, None), P())
    return jax.shard_map(
        tuned_body if tuned else plain_body,
        mesh=mesh,
        in_specs=placed,
        out_specs=(P(BOTH, None), P()),
        check_vma=False,
    )
```

```python
import functools

import jax
import jax.numpy as jnp
from jax import lax
from jax.experimental import pallas as pl
from jax.experimental.pallas import tpu as pltpu
from jax.sharding import PartitionSpec as P

F32 = jnp.float32
BF16 = jnp.bfloat16
LANES = 128
NT = (((1,), (1,)), ((), ()))
NN = (((1,), (0,)), ((), ()))
BOTH = ("row", "col")
RING = (0, 2, 4, 6, 7, 5, 3, 1)
SPREAD = (0, 2, 1, 3)
RING_AT = tuple(RING.index(r) for r in range(8))

dot32 = functools.partial(lax.dot_general, preferred_element_type=F32)
dot_exact = functools.partial(
    lax.dot_general, precision=lax.Precision.HIGHEST, preferred_element_type=F32
)


def split(values):
    high = values.astype(BF16)
    return high, (values - high.astype(F32)).astype(BF16)


def pick(table, index):
    return jnp.asarray(table, jnp.int32)[index]


def after(value, *others):
    return lax.optimization_barrier((value, others))[0]


SLOTS = 3
ROUND = 32


def stream(source_ref, slots, sems, steps, corner, prepare, use):
    _, height, width = slots.shape

    def copy(step):
        row0, col0 = corner(step)
        slot = lax.rem(step, SLOTS)
        rows = pl.ds(pl.multiple_of(row0, ROUND), height)
        cols = pl.ds(pl.multiple_of(col0, LANES), width)
        return pltpu.make_async_copy(source_ref.at[rows, cols], slots.at[slot], sems.at[slot])

    copy(jnp.int32(0)).start()
    prepare()
    for step in range(1, min(SLOTS - 1, steps)):
        copy(jnp.int32(step)).start()

    def one(step, carry):
        @pl.when(step + SLOTS - 1 < steps)
        def _():
            copy(step + SLOTS - 1).start()

        copy(step).wait()
        use(step, lax.rem(step, SLOTS))
        return carry

    lax.fori_loop(0, steps, one, 0)


def unit_start(place, aways, index, blocks):
    away = jnp.int32(aways[0])
    for i, a in enumerate(aways[1:], 1):
        away = jnp.where(index == i, a, away)
    return lax.rem(place + away + 8, 8) * blocks // 8 * LANES


def take_center(slots, slot, center, row0, col0, offset):
    _, height, width = slots.shape
    first = col0 - row0 - offset

    @pl.when((offset >= 0) & (first < height) & (first + width > 0))
    def _():
        rows = lax.broadcasted_iota(jnp.int32, (ROUND, LANES), 0)
        cols = lax.broadcasted_iota(jnp.int32, (ROUND, LANES), 1)

        def tile(index, carry):
            for part in range(LANES // ROUND):
                at = first + index * LANES + part * ROUND

                @pl.when((at >= 0) & (at < height))
                def _():
                    here = (slot, pl.ds(pl.multiple_of(at, ROUND), ROUND), pl.ds(pl.multiple_of(index * LANES, LANES), LANES))
                    slots[here] = slots[here] - jnp.where(rows + part * ROUND == cols, center, 0.0)

            return carry

        lax.fori_loop(0, width // LANES, tile, 0)


VMEM = pl.BlockSpec(memory_space=pltpu.VMEM)
SMEM = pl.BlockSpec(memory_space=pltpu.SMEM)
ANY = pl.BlockSpec(memory_space=pl.ANY)


def kernel_params(count, chunks, depth, width, vectors):
    return dict(
        compiler_params=pltpu.CompilerParams(vmem_limit_bytes=36 * 2**20),
        cost_estimate=pl.CostEstimate(
            flops=6 * count * chunks * depth * width * vectors,
            bytes_accessed=4 * count * chunks * depth * width,
            transcendentals=0,
        ),
    )


def bring(pieces, refs, held, sems):
    copies, rest = [], list(refs)
    for i, group in enumerate(pieces):
        at, own = 0, []
        for q, piece in enumerate(group):
            own.append(pltpu.make_async_copy(rest.pop(0), held.at[i, pl.ds(at, piece.shape[0])], sems.at[i, q]))
            at += piece.shape[0]
        copies.append(own)
    return copies


def columns_product(laplacian, scalars, center, panel, aways, depth, width, first_chunk=0, totals=None):
    count, chunks = len(aways), len(panel)
    lanes = panel[0][0].shape[1]
    vectors, per = sum(p.shape[0] for p in panel[0]), len(panel[0])
    blocks = laplacian.shape[1] // LANES
    given = [] if totals is None else [totals]

    def kernel(scalars_ref, center_ref, tile_ref, *refs):
        piece_refs, total_refs = refs[: per * chunks], refs[per * chunks : per * chunks + len(given)]
        out_ref, slots, panel_ref, high_ref, low_ref, sum_ref, total_buf, sems, in_sems, total_sem, out_sems = refs[-11:]
        copies = bring(panel, piece_refs, panel_ref, in_sems)
        more = [pltpu.make_async_copy(r, total_buf, total_sem.at[0]) for r in total_refs]

        def corner(step):
            chunk = lax.bitwise_xor(first_chunk + lax.rem(step, chunks), scalars_ref[2])
            return chunk * depth, unit_start(scalars_ref[0], aways, step // chunks, blocks)

        def prepare():
            for copy in [c for own in copies for c in own] + more:
                copy.start()

        def use(step, slot):
            chunk, unit = lax.rem(step, chunks), step // chunks
            for c in range(chunks):

                @pl.when(step == c)
                def _(c=c):
                    for copy in copies[c]:
                        copy.wait()
                    high, low = split(panel_ref[c, :, :depth])
                    high_ref[c] = high
                    low_ref[c] = low

            row0, col0 = corner(step)
            take_center(slots, slot, center_ref[0], row0, col0, scalars_ref[1])
            high, low = split(slots[slot])
            z_high, z_low = high_ref[chunk], low_ref[chunk]
            term = dot32(z_high, high, NN) + dot32(z_low, high, NN) + dot32(z_high, low, NN)

            @pl.when(chunk == 0)
            def _():
                if more:

                    @pl.when(step == 0)
                    def _():
                        for copy in more:
                            copy.wait()

                    sum_ref[unit] = total_buf[unit] + term
                else:
                    sum_ref[unit] = term

            @pl.when(chunk > 0)
            def _():
                sum_ref[unit] += term

            @pl.when(chunk == chunks - 1)
            def _():
                pltpu.make_async_copy(sum_ref.at[unit], out_ref.at[unit], out_sems.at[unit]).start()

        stream(tile_ref, slots, sems, count * chunks, corner, prepare, use)
        for unit in range(count):
            pltpu.make_async_copy(sum_ref.at[unit], out_ref.at[unit], out_sems.at[unit]).wait()

    return pl.pallas_call(
        kernel,
        out_shape=jax.ShapeDtypeStruct((count, vectors, width), F32),
        in_specs=[SMEM, SMEM, ANY] + [ANY] * (per * chunks + len(given)),
        out_specs=ANY,
        scratch_shapes=[
            pltpu.VMEM((SLOTS, depth, width), F32),
            pltpu.VMEM((chunks, vectors, lanes), F32),
            pltpu.VMEM((chunks, vectors, depth), BF16),
            pltpu.VMEM((chunks, vectors, depth), BF16),
            pltpu.VMEM((count, vectors, width), F32),
            pltpu.VMEM((count, vectors, width) if given else (1, 8, LANES), F32),
            pltpu.SemaphoreType.DMA((SLOTS,)),
            pltpu.SemaphoreType.DMA((chunks, per)),
            pltpu.SemaphoreType.DMA((1,)),
            pltpu.SemaphoreType.DMA((count,)),
        ],
        name="columns_product",
        **kernel_params(count, chunks, depth, width, vectors),
    )(scalars, center, laplacian, *[p for pieces in panel for p in pieces], *given)


def rows_product(laplacian, scalars, center, units, aways, totals, chunks, depth, lanes):
    count, number = len(units), len(chunks)
    width = units[0][0].shape[1]
    vectors = sum(p.shape[0] for p in units[0])
    per = max(len(group) for group in units)
    flat = [p for pieces in units for p in pieces]
    blocks = laplacian.shape[1] // LANES
    given = [] if totals is None else [totals]
    skip = chunks[0] if given and totals.shape[0] > number else 0

    def kernel(scalars_ref, center_ref, tile_ref, *refs):
        total_refs = refs[len(flat) : len(flat) + len(given)]
        out_ref, slots, unit_ref, high_ref, low_ref, sum_ref, total_buf, sems, in_sems, total_sems, out_sems = refs[-11:]
        copies = bring(units, refs[: len(flat)], unit_ref, in_sems)

        def total(chunk):
            return [pltpu.make_async_copy(r.at[skip + chunk], total_buf.at[chunk], total_sems.at[chunk]) for r in total_refs]

        def corner(step):
            first = (chunks[0] + step // count) * depth
            return first, unit_start(scalars_ref[0], aways, lax.rem(step, count), blocks)

        def prepare():
            for copy in [c for own in copies for c in own] + [c for i in range(number) for c in total(i)]:
                copy.start()

        def use(step, slot):
            chunk, unit = step // count, lax.rem(step, count)
            for u in range(count):

                @pl.when(step == u)
                def _(u=u):
                    for copy in copies[u]:
                        copy.wait()
                    high, low = split(unit_ref[u])
                    high_ref[u] = high
                    low_ref[u] = low
                    if u == 0 and lanes > depth:
                        sum_ref[:, :, depth:] = jnp.zeros((number, vectors, lanes - depth), F32)

            row0, col0 = corner(step)
            take_center(slots, slot, center_ref[0], row0, col0, scalars_ref[1])
            high, low = split(slots[slot])
            z_high, z_low = high_ref[unit], low_ref[unit]
            term = dot32(z_high, high, NT) + dot32(z_low, high, NT) + dot32(z_high, low, NT)

            @pl.when(unit == 0)
            def _():
                if given:
                    for copy in total(chunk):
                        copy.wait()
                    sum_ref[chunk, :, :depth] = total_buf[chunk, :, :depth] + term
                else:
                    sum_ref[chunk, :, :depth] = term

            @pl.when(unit > 0)
            def _():
                sum_ref[chunk, :, :depth] += term

            @pl.when(unit == count - 1)
            def _():
                pltpu.make_async_copy(sum_ref.at[chunk], out_ref.at[chunk], out_sems.at[chunk]).start()

        stream(tile_ref, slots, sems, count * number, corner, prepare, use)
        for chunk in range(number):
            pltpu.make_async_copy(sum_ref.at[chunk], out_ref.at[chunk], out_sems.at[chunk]).wait()

    return pl.pallas_call(
        kernel,
        out_shape=jax.ShapeDtypeStruct((number, vectors, lanes), F32),
        in_specs=[SMEM, SMEM, ANY] + [ANY] * (len(flat) + len(given)),
        out_specs=ANY,
        scratch_shapes=[
            pltpu.VMEM((SLOTS, depth, width), F32),
            pltpu.VMEM((count, vectors, width), F32),
            pltpu.VMEM((count, vectors, width), BF16),
            pltpu.VMEM((count, vectors, width), BF16),
            pltpu.VMEM((number, vectors, lanes), F32),
            pltpu.VMEM((number, vectors, lanes) if given else (1, 8, LANES), F32),
            pltpu.SemaphoreType.DMA((SLOTS,)),
            pltpu.SemaphoreType.DMA((count, per)),
            pltpu.SemaphoreType.DMA((number,)),
            pltpu.SemaphoreType.DMA((number,)),
        ],
        name="rows_product",
        **kernel_params(count, number, depth, width, vectors),
    )(scalars, center, laplacian, *flat, *given)


def inverse_factor(gram):
    size = gram.shape[0]
    tall = 32

    def kernel(gram_ref, out_ref, work):
        work[...] = gram_ref[...]
        lane = lax.broadcasted_iota(jnp.int32, (1, size), 1)
        below = lax.broadcasted_iota(jnp.int32, (tall, 1), 0)
        for first in range(0, size, tall):
            rows = work[first : first + tall]
            for q in range(0, tall, 2):
                k = first + q
                col1 = jnp.broadcast_to(rows[:, k : k + 1], rows.shape)
                col2 = jnp.broadcast_to(rows[:, k + 1 : k + 2], rows.shape)
                over1 = lax.rsqrt(col1[q : q + 1])
                cross = col2[q : q + 1] * over1
                over2 = lax.rsqrt(col2[q + 1 : q + 2] - cross * cross)
                row1 = jnp.where(lane == k, 1.0, jnp.where(lane == k + 1, 0.0, rows[q : q + 1])) * over1
                row2 = jnp.where(lane == k + 1, 1.0, jnp.where(lane == k, 0.0, rows[q + 1 : q + 2]))
                row2 = (row2 - cross * row1) * over2
                times1 = col1 * over1
                times2 = (col2 - times1 * cross) * over2
                kept = jnp.where((lane == k) | (lane == k + 1), 0.0, rows)
                rows = jnp.where(
                    below > q + 1,
                    kept - times1 * row1 - times2 * row2,
                    jnp.where(below == q, row1, jnp.where(below == q + 1, row2, rows)),
                )
            rows = jnp.where((lane > first + below) & (lane < first + tall), 0.0, rows)
            work[first : first + tall] = rows
            rest = first + tall
            if rest < size:
                skip = rest // LANES * LANES
                update = dot_exact(rows[:, skip:], rows, (((0,), (0,)), ((), ())))
                done = (lane >= first) & (lane < rest)
                work[rest:] = jnp.where(done, 0.0, work[rest:]) - update[rest - skip :]
        at_row = lax.broadcasted_iota(jnp.int32, (size, size), 0)
        at_lane = lax.broadcasted_iota(jnp.int32, (size, size), 1)
        out_ref[...] = jnp.where(at_lane <= at_row, work[...], 0.0)

    return pl.pallas_call(
        kernel,
        out_shape=jax.ShapeDtypeStruct((size, size), F32),
        in_specs=[VMEM],
        out_specs=VMEM,
        scratch_shapes=[pltpu.VMEM((size, size), F32)],
        cost_estimate=pl.CostEstimate(flops=2 * size**3, bytes_accessed=8 * size**2, transcendentals=2 * size),
        name="inverse_factor",
    )(gram)


def swap(values, axis, mask):
    size = lax.axis_size(axis)
    return lax.ppermute(values, axis, [(i, i ^ mask) for i in range(size)])


def around(values, way):
    return lax.ppermute(values, "row", [(RING[p], RING[(p + way) % 8]) for p in range(8)])


def sum_stages(partial):
    row, col = lax.axis_index("row"), lax.axis_index("col")
    stages = (("col", 1, col & 1), ("col", 2, (col >> 1) & 1), ("row", 1, row & 1))
    values = partial
    for axis, mask, bit in stages:
        half = values.shape[0] // 2
        low, high = values[:half], values[half:]
        keep = jnp.where(bit == 0, low, high)
        send = jnp.where(bit == 0, high, low)
        values = keep + swap(send, axis, mask)
        yield values
    terms = [values] + [swap(values, "row", mask) for mask in (2, 4, 6)]
    z = row >> 1
    ordered = []
    for place in range(4):
        which = z ^ place
        ordered.append(jnp.where(which == 0, terms[0], jnp.where(which == 1, terms[1], jnp.where(which == 2, terms[2], terms[3]))))
    values = (ordered[0] + ordered[1]) + (ordered[2] + ordered[3])
    yield values
    for axis, mask, bit in reversed(stages):
        other = swap(values, axis, mask)
        low = jnp.where(bit == 0, values, other)
        high = jnp.where(bit == 0, other, values)
        values = jnp.concatenate([low, high], axis=0)
        yield values


def tuned_body(laplacian, block, bounds):
    tile_rows, tile_cols = laplacian.shape
    own_rows, vectors = block.shape
    half = vectors // 2
    depth = tile_rows // 2
    lanes = -(-depth // LANES) * LANES
    row, col = lax.axis_index("row"), lax.axis_index("col")
    core, x_at = col & 1, col >> 1
    place = pick(RING_AT, row)
    blocks = tile_cols // LANES
    starts = tuple(blocks * p // 8 for p in range(9))
    width = LANES * max(b - a for a, b in zip(starts, starts[1:]))
    center = (bounds[1] + bounds[0]) * 0.5
    half_width = (bounds[1] - bounds[0]) * 0.5
    factor_two = 2.0 / half_width
    centers = center.reshape(1)
    valid = lax.broadcasted_iota(jnp.int32, (1, width), 1) < (pick(starts, place + 1) - pick(starts, place)) * LANES
    per_tile = tile_cols // tile_rows
    offset = jnp.where(row // per_tile == col, (row % per_tile) * tile_rows, -1)
    scalars, turned_scalars = (jnp.stack([place, offset, f]).astype(jnp.int32) for f in (jnp.int32(0), x_at))

    def through_columns(here, rest, scalars=scalars, before=None):
        def product(call, aways, panel, made=(), **more):
            told = scalars if before is None else after(scalars, *before(call, *made))
            return columns_product(laplacian, told, centers, panel, aways, depth, width, **more)

        begun_far = product(0, (4,), [here])
        begun = product(0, (3, -3), [here])
        there = rest(begun_far, begun)
        panel = [here, there]
        far = product(1, (4,), [there], first_chunk=1, totals=begun_far)[0]
        right, left = around(far[:half], 1), around(far[half:], -1)
        ahead, behind = product(2, (3, -3), [there], first_chunk=1, totals=begun, made=(far,))
        ahead = jnp.concatenate([ahead[:half] + right, ahead[half:]], 0)
        behind = jnp.concatenate([behind[:half], behind[half:] + left], 0)
        right, left = around(ahead, 1), around(behind, -1)
        ahead, behind = product(3, (2, -2), panel)
        right, left = around(ahead + right, 1), around(behind + left, -1)
        ahead, behind, own = product(4, (1, -1, 0), panel)
        ahead, behind = ahead + right, behind + left
        return panel, (own, around(ahead, 1), around(behind, -1)), ahead

    def through_rows(unit, before):
        unit = jnp.where(valid, unit, 0.0)

        def product(aways, units, totals, chunks):
            return rows_product(laplacian, scalars, centers, units, aways, totals, chunks, depth, lanes)

        right, left = around(unit, 1), around(unit, -1)
        totals = product((0,), [[unit]], None, (0, 1))
        right, left = after(right, totals), after(left, totals)
        right2, left2 = around(right, 1), around(left, -1)
        totals = product((-1, 1), [[right], [left]], totals, (0, 1))
        right2, left2 = after(right2, totals), after(left2, totals)
        right3, left3 = around(right2, 1), around(left2, -1)
        totals = product((-2, 2), [[right2], [left2]], totals, (0, 1))
        right3, left3 = after(right3, totals), after(left3, totals)
        far = [around(right3[:half], 1), around(left3[half:], -1)]
        first = product((-3, 3), [[right3], [left3]], totals, (0,))
        first = product((4,), [far], first, (0,))[0]
        first = first[:half] + swap(first[half:], "col", 1)
        second = product((-3, 3, 4), [[right3], [left3], far], after(totals, first), (1,))[0]
        first = factor_two * (first + swap(first, "col", 2)) - before[0][0]
        second = after(second[:half] + swap(second[half:], "col", 1), first)
        second_there = swap(second, "col", 2)

        def rest(*others):
            new = after(factor_two * (second + second_there) - before[1][0], *others)
            return new, swap(new, "col", 1)

        return (first, swap(first, "col", 1)), rest

    away_block = swap(block, "col", 2)

    def turned(pair):
        mine, other = pair[0].T, pair[1].T
        both = jnp.where(core == 0, jnp.concatenate([mine, other], 1), jnp.concatenate([other, mine], 1))
        both = jnp.pad(both, ((0, 0), (0, lanes - depth)))
        return jnp.where(core == 0, both[:half], both[half:]), jnp.where(core == 0, both[half:], both[:half])

    def rest(*others):
        away = after(away_block, *others)
        return turned([away, swap(away, "col", 1)])

    here = turned([block, swap(block, "col", 1)])
    (_, there), terms, _ = through_columns(here, rest, turned_scalars)
    panel = [(jnp.where(x_at == 0, here[0], there[0]),), (jnp.where(x_at == 0, there[0], here[0]),)]
    filter_one = sum(terms) / half_width
    panel_two, terms, _ = through_columns(*through_rows(filter_one, panel))
    filter_three = factor_two * sum(terms) - filter_one

    def straight(pieces):
        mine, other = pieces
        return jnp.where(core == 0, jnp.concatenate([mine, other], 0), jnp.concatenate([other, mine], 0))

    here, rest = through_rows(filter_three, panel_two)
    held, got = [], []
    lead = LANES
    over = tile_rows - starts[4] * LANES

    def rest_kept(*others):
        got.append(rest(*others))
        return got[0]

    def before(call, *made):
        if call == 2:
            chunks = [straight(pair)[:, :depth] for pair in after((here, got[0]), *made)]
            chunk = jnp.where(x_at == 0, chunks[0], chunks[1])
            own = jnp.where(core == 0, chunk[:, :own_rows], chunk[:, own_rows:])
            held.append(sum_stages(dot_exact(own, own, NT)))
            padded = jnp.concatenate([jnp.zeros((vectors, lead), F32)] + chunks, 1)
            part = row % per_tile
            send_from = pick(starts, 4 * part + pick(SPREAD, col)) * LANES - part * tile_rows + lead
            sent = lax.dynamic_slice_in_dim(padded, send_from, width, 1)
            got.extend([own, sent, chunks[1][:, depth - over :]])
        for _ in range((0, 0, 0, 2, 3)[call]):
            held.append(next(held[0]))
        return [] if call < 3 else held[-1:] + (got[2:] if call == 4 else [])

    _, (image, from_left, from_right), last_sent = through_columns(here, rest_kept, before=before)
    _, own, sent, sent_head = got
    filtered = own.T
    sent, sent_head = after((sent, sent_head), last_sent)
    pairs = [
        (4 * r + c, 4 * RING[4 * (r % per_tile) + SPREAD[c]] + r // per_tile) for r in range(8) for c in range(4)
    ]
    moved = lax.ppermute(sent, BOTH, pairs)
    head = lax.ppermute(sent_head, BOTH, [(4 * (per_tile * c), 4 * RING[4] + c) for c in range(4)])
    moved = jnp.where(valid, moved + jnp.pad(head, ((0, 0), (0, width - over))), 0.0)

    *_, gram = held[0]
    inverse = inverse_factor(after(gram, last_sent))
    image = after(image, inverse) + from_left + from_right
    image = straight((image[:half], image[half:]))
    *_, projected = sum_stages(dot_exact(moved, image, NT))
    projected = projected + center * gram
    projected = (projected + projected.T) * 0.5
    rayleigh = dot_exact(dot_exact(inverse, projected, NN), inverse, NT)
    return (filtered, rayleigh)


def plain_body(laplacian, block, bounds):
    row_index = lax.axis_index("row")
    col_index = lax.axis_index("col")
    tile_rows, tile_cols = laplacian.shape
    center = (bounds[1] + bounds[0]) * 0.5
    half_width = (bounds[1] - bounds[0]) * 0.5
    factor_two = 2.0 / half_width
    global_rows = row_index * tile_rows + lax.broadcasted_iota(jnp.int32, (tile_rows, tile_cols), 0)
    global_cols = col_index * tile_cols + lax.broadcasted_iota(jnp.int32, (tile_rows, tile_cols), 1)
    moved_diagonal = laplacian - center * (global_rows == global_cols).astype(F32)

    def through_columns(values):
        panel = lax.all_gather(values, "col", axis=0, tiled=True)
        out = dot_exact(moved_diagonal, panel, (((0,), (0,)), ((), ())))
        return lax.psum_scatter(out, "row", scatter_dimension=0, tiled=True)

    def through_rows(values):
        panel = lax.all_gather(values, "row", axis=0, tiled=True)
        out = dot_exact(moved_diagonal, panel, NN)
        return lax.psum_scatter(out, "col", scatter_dimension=0, tiled=True)

    filter_one = through_columns(block) / half_width
    filter_two = factor_two * through_rows(filter_one) - block
    filter_three = factor_two * through_columns(filter_two) - filter_one
    filter_four = factor_two * through_rows(filter_three) - filter_two
    image = through_columns(filter_four)
    rows, cols = lax.axis_size("row"), lax.axis_size("col")
    pairs = [(i, (i % rows) * cols + i // rows) for i in range(rows * cols)]
    moved = lax.ppermute(filter_four, BOTH, pairs)
    inner = (((0,), (0,)), ((), ()))
    gram, projected = lax.psum((dot_exact(moved, moved, inner), dot_exact(moved, image, inner)), BOTH)
    projected = projected + center * gram
    projected = (projected + projected.T) * 0.5
    factor = jnp.linalg.cholesky(gram)
    first_solve = jax.scipy.linalg.solve_triangular(factor, projected, lower=True)
    rayleigh = jax.scipy.linalg.solve_triangular(factor, first_solve.T, lower=True)
    return (filter_four, rayleigh)


def solution(mesh):
    tuned = mesh.shape["row"] == 8 and mesh.shape["col"] == 4
    placed = (P("row", "col"), P(BOTH, None), P())
    return jax.shard_map(
        tuned_body if tuned else plain_body,
        mesh=mesh,
        in_specs=placed,
        out_specs=(P(BOTH, None), P()),
        check_vma=False,
    )
```
